32 devices in a mesh: groups: 2 (over y), blk: 4 (over z), sub: 4 (over x, core).
Axes of the slice: x: 2, y: 2, z: 4, core: 2. Of those that a mesh axis runs over, the one named last changes fastest.
Arguments:
- dense_coef: float32 [256, 128, 128], P(('groups', 'blk'), 'sub'), parts along dimension 0, may hold values from -6 to 6
- sparse_coef: float32 [8, 128, 128], P(('groups', 'blk'), 'sub'), parts along dimension 0, may hold values from -0.0234375 to 0.0234375
- pattern: int32 [8], P('groups'), parts along dimension 0, may hold values from 0 to 159, as said below
Outputs:
- product_coef: float32 [256, 128, 128], P(('groups', 'blk'), 'sub'), parts along dimension 0
The draws below stay inside these ranges and needn't reach their ends.
There are 2 independent parts, one for each index of `groups`. The reference program is written for one: setup_inputs(seed, part) draws one part's arguments, and reference() takes and returns one part's arrays. A program takes and returns all parts, laid end to end along the dimension named above; each array names one. Nothing has to cross between parts.
Inputs may be any that keep to these rules, and one draw needn't show every extreme that they name: `pattern`: the 4 entries are distinct.
All inputs are finite; a program needn't handle non-finite values.
Results may differ from the reference program's by a relative error of at most 0.000076.
Values sent between devices are 32-bit elements; how exact they have to be, the bound alone decides.
A program may use at most 128 MiB of HBM per device.

```python
import jax
import jax.numpy as jnp

ROWS = 128
Q = 128
L = 16384
NT = 128
SB = 160
NNZ = 4


def draw_pattern(key, part):
    order = jax.random.permutation(jax.random.fold_in(key, 7), SB)
    return order[:NNZ].astype(jnp.int32)


def level_of(rng, dims, shards, low, high):
    gain, own = 1.0, jax.random.fold_in(rng, 6)
    for position, parts in shards:
        steps = jnp.exp(jax.random.uniform(jax.random.fold_in(own, position), (parts,), jnp.float32, low / len(shards), high / len(shards)))
        gain = gain * jnp.repeat(steps, dims[position] // parts).reshape([-1 if axis == position else 1 for axis in range(len(dims))])
    return gain


def normal_values(stream_key, shape, scale, limit, split=(), kind=jnp.bfloat16):
    values = scale * jax.random.normal(stream_key, shape, jnp.float32)
    if split:
        values = values * level_of(stream_key, shape, split, -0.22, 0.18)
    return jnp.clip(values, -limit, limit).astype(kind)


def setup_inputs(seed: int = 0, part: int = 0) -> dict:
    streams_of = jax.random.split(jax.random.key(seed), 4)
    own_keys = jax.random.split(jax.random.fold_in(streams_of[3], part), 4)
    dense_coef = normal_values(own_keys[0], (NT, Q, ROWS), 1.0, 6.0, ((0, 4), (1, 4)), jnp.float32)
    sparse_coef = normal_values(own_keys[1], (NNZ, Q, ROWS), (NNZ * L) ** -0.5, 0.0234375, ((0, 4), (1, 4)), jnp.float32)
    pattern = draw_pattern(jax.random.fold_in(jax.random.fold_in(streams_of[3], part), 71), part)
    return {"dense_coef": dense_coef, "sparse_coef": sparse_coef, "pattern": pattern}


def reference(dense_coef, sparse_coef, pattern):
    block_total = dense_coef.shape[0]
    length = ROWS * Q
    dense_flat = jnp.transpose(dense_coef, (0, 2, 1)).reshape(block_total, length)
    sparse_flat = jnp.transpose(sparse_coef, (0, 2, 1)).reshape(sparse_coef.shape[0], length)
    dense_spec = jnp.fft.rfft(dense_flat, n=2 * length, axis=1)
    sparse_spec = jnp.fft.rfft(sparse_flat, n=2 * length, axis=1)
    block_ids = jnp.arange(block_total, dtype=jnp.int32)
    summed = jnp.zeros_like(dense_spec)
    for entry in range(sparse_coef.shape[0]):
        source = jnp.mod(block_ids - pattern[entry].astype(jnp.int32), block_total).astype(jnp.int32)
        summed = summed + jnp.take(dense_spec, source, axis=0) * sparse_spec[entry][None, :]
    product = jnp.fft.irfft(summed, n=2 * length, axis=1)
    result = product[:, :length] + jnp.roll(product[:, length:], 1, axis=0)
    return jnp.transpose(result.reshape(block_total, ROWS, Q), (0, 2, 1)).astype(jnp.float32)
```

```python
import numpy as np

import jax
import jax.numpy as jnp
from jax import lax
from jax.experimental import pallas as pl
from jax.experimental.pallas import tpu as pltpu
from jax.sharding import PartitionSpec as P

NN = (((1,), (0,)), ((), ()))
NT = (((1,), (1,)), ((), ()))


def halves(x):
    hi = x.astype(jnp.bfloat16)
    return hi, (x - hi.astype(jnp.float32)).astype(jnp.bfloat16)


def dot3(a, b, dims):
    def one(x, y):
        return lax.dot_general(x, y, dims, preferred_element_type=jnp.float32)

    return one(a[0], b[0]) + (one(a[0], b[1]) + one(a[1], b[0]))


def tables(rows, cols, devices, chunk):
    per = rows // devices
    e = np.arange(rows)
    phase = (np.outer(2 * e + 1, np.arange(rows)) % (4 * rows)) * (2 * np.pi / (4 * rows))
    both = np.stack([np.cos(phase), -np.sin(phase)], axis=1)
    by_device = both.reshape(devices, per // chunk, chunk, 2, rows)
    row_table = by_device.transpose(1, 0, 2, 3, 4).reshape(2 * rows, rows)
    sparse_rows = max(8, 2 * per)
    sparse_table = np.zeros((devices, sparse_rows, rows))
    sparse_table[:, : 2 * per] = both.reshape(devices, 2 * per, rows)
    twist_phase = np.outer(np.arange(cols), 2 * e + 1) * (2 * np.pi / (4 * rows * cols))
    twist = np.stack([np.cos(twist_phase), -np.sin(twist_phase)], axis=2)
    twist = twist.reshape(cols, devices, 2 * per).transpose(1, 0, 2)
    dft_phase = (np.outer(np.arange(cols), np.arange(cols)) % cols) * (2 * np.pi / cols)
    dft = np.concatenate([np.cos(dft_phase), -np.sin(dft_phase)], axis=1)
    out = (row_table, sparse_table.reshape(devices * sparse_rows, rows), twist, dft)
    return [np.asarray(t, np.float32) for t in out]


def kernel(
    nz, ns, chunk,
    dense, sparse, pattern, row_table, sparse_table, twist_all, dft,
    out,
    y, r, u, v, ysp, rsp, xs, twist,
    send1, recv1, send2, recv2, send3, recv3, twist_sem,
):
    devices = nz * ns
    blocks, qlocal, rows = dense.shape
    cols = qlocal * ns
    groups = cols // qlocal
    deep = blocks // groups
    per = rows // devices
    chunks = per // chunk
    total = blocks * nz
    span = chunk * 2 * deep
    sparse_rows = rsp.shape[1] // devices
    entries = sparse.shape[0]
    iz, js = lax.axis_index("blk"), lax.axis_index("sub")
    me = iz * ns + js

    get_twist = pltpu.make_async_copy(twist_all.at[me], twist, twist_sem)
    get_twist.start()

    def where(i):
        peer = lax.rem(me + i, devices)
        return peer, {"blk": peer // ns, "sub": lax.rem(peer, ns)}

    barrier = pltpu.get_barrier_semaphore()

    @pl.loop(1, devices)
    def _(i):
        pl.semaphore_signal(
            barrier, inc=1, device_id=where(i)[1], device_id_type=pl.DeviceIdType.MESH
        )

    for i in range(entries):
        wide = jnp.concatenate([sparse[i]] * groups, axis=0)
        ysp[i] = dot3(halves(sparse_table[...]), halves(wide), NT)

    pl.semaphore_wait(barrier, devices - 1)

    def at(ref, ch, dev):
        return ref.at[pl.ds(pl.multiple_of((ch * devices + dev) * span, span), span), :]

    def move(src, dst, sends, recvs, ch, i):
        peer, ident = where(i)
        return pltpu.make_async_remote_copy(
            src_ref=at(src, ch, peer), dst_ref=at(dst, ch, me),
            send_sem=sends.at[ch, i], recv_sem=recvs.at[ch, i],
            device_id=ident, device_id_type=pl.DeviceIdType.MESH,
        )

    def move_sparse(n, i):
        peer, ident = where(i)

        def part(ref, dev):
            start = pl.multiple_of(dev * sparse_rows, sparse_rows)
            return ref.at[n, pl.ds(start, sparse_rows), :]

        return pltpu.make_async_remote_copy(
            src_ref=part(ysp, peer), dst_ref=part(rsp, me),
            send_sem=send3.at[n, i], recv_sem=recv3.at[n, i],
            device_id=ident, device_id_type=pl.DeviceIdType.MESH,
        )

    for n in range(entries):
        @pl.loop(1, devices)
        def _(i):
            move_sparse(n, i).start()
        own = pl.ds(pl.multiple_of(me * sparse_rows, sparse_rows), sparse_rows)
        rsp[n, own, :] = ysp[n, own, :]

    inputs = []
    for j in range(deep):
        inputs.append(halves(jnp.concatenate([dense[g * deep + j] for g in range(groups)], axis=0)))
    slab = devices * chunk * 2
    for ch in range(chunks):
        weights = halves(row_table[ch * slab:(ch + 1) * slab, :])
        for j in range(deep):
            y[pl.ds(ch * slab * deep + j, slab, stride=deep), :] = dot3(weights, inputs[j], NT)

        @pl.loop(1, devices)
        def _(i):
            move(y, r, send1, recv1, ch, i).start()
        own = pl.ds(pl.multiple_of((ch * devices + me) * span, span), span)
        r[own, :] = y[own, :]

    get_twist.wait()
    for n in range(entries):
        @pl.loop(1, devices)
        def _(i):
            move_sparse(n, i).wait()

    group_of = lax.broadcasted_iota(jnp.int32, (deep, cols), 1) // qlocal
    sub_group = lax.broadcasted_iota(jnp.int32, (ns, cols), 1) // qlocal
    sub_row = lax.broadcasted_iota(jnp.int32, (ns, cols), 0)
    own_lane = sub_group == sub_row

    def regroup(tiles):
        result = []
        for b in range(groups):
            got = None
            for a in range(groups):
                shift = ((a - b) * qlocal) % cols
                piece = pltpu.roll(tiles[a], shift, 1) if shift else tiles[a]
                got = piece if got is None else jnp.where(group_of == a, piece, got)
            result.append(got)
        return result

    for ch in range(chunks):
        @pl.loop(1, devices)
        def _(i):
            move(y, r, send1, recv1, ch, i).wait()

        for e in range(chunk):
            k = ch * chunk + e
            base = (e * 2) * deep
            for c in range(2):
                for z in range(nz):
                    tiles = []
                    for s in range(ns):
                        start = (ch * devices + z * ns + s) * span + base + c * deep
                        tiles.append(r[start:start + deep, :])
                    for g, tile in enumerate(regroup(tiles)):
                        start = z * blocks + g * deep
                        xs[start:start + deep, c * cols:(c + 1) * cols] = tile
            spectra = []
            for z in range(nz):
                for n in range(entries):
                    pair = []
                    for c in range(2):
                        start = z * ns * sparse_rows + 2 * k + c
                        got = rsp[n, pl.ds(start, ns, stride=sparse_rows), :]
                        pair.append(jnp.sum(jnp.where(own_lane, got, 0.0), axis=0, keepdims=True))
                    spectra.append(jnp.concatenate(pair, axis=1))
            count = len(spectra)
            fill = -count % 8
            if fill:
                spectra.append(jnp.zeros((fill, 2 * cols), jnp.float32))
            spectra = jnp.concatenate(spectra, axis=0)

            cos_q = twist[:, 2 * k:2 * k + 1]
            sin_q = twist[:, 2 * k + 1:2 * k + 2]
            base_re, base_im = dft[:, :cols], dft[:, cols:]
            t_re = cos_q * base_re - sin_q * base_im
            t_im = cos_q * base_im + sin_q * base_re
            matrix = halves(
                jnp.concatenate(
                    [
                        jnp.concatenate([t_re, t_im], axis=1),
                        jnp.concatenate([-t_im, t_re], axis=1),
                    ],
                    axis=0,
                )
            )

            x = xs[...]
            before = pltpu.roll(x, 1, 0)
            parity = lax.rem(me * per + k, 2)
            sign = (1 - 2 * parity).astype(jnp.float32)
            turned = jnp.concatenate([-before[:, cols:], before[:, :cols]], axis=1)
            spectrum = dot3(halves(x + sign * turned), matrix, NN)
            sparse_spectrum = dot3(halves(spectra), matrix, NN)
            sum_re = jnp.zeros((total, cols), jnp.float32)
            sum_im = jnp.zeros((total, cols), jnp.float32)
            for n in range(count):
                shift = lax.rem(pattern[n], total)
                a = pltpu.roll(spectrum, shift, 0)
                s_re = sparse_spectrum[n:n + 1, :cols]
                s_im = sparse_spectrum[n:n + 1, cols:]
                sum_re += a[:, :cols] * s_re - a[:, cols:] * s_im
                sum_im += a[:, :cols] * s_im + a[:, cols:] * s_re
            back = dot3(halves(jnp.concatenate([sum_re, sum_im], axis=1)), matrix, NT)
            for c in range(2):
                for z in range(nz):
                    tiles = []
                    for g in range(groups):
                        start = z * blocks + g * deep
                        tiles.append(back[start:start + deep, c * cols:(c + 1) * cols])
                    for s, tile in enumerate(regroup(tiles)):
                        start = (ch * devices + z * ns + s) * span + base + c * deep
                        u[start:start + deep, :] = tile

        @pl.loop(1, devices)
        def _(i):
            move(u, v, send2, recv2, ch, i).start()
        own = pl.ds(pl.multiple_of((ch * devices + me) * span, span), span)
        v[own, :] = u[own, :]

    for ch in range(chunks):
        @pl.loop(1, devices)
        def _(i):
            move(u, v, send2, recv2, ch, i).wait()

    weights = halves(row_table[...])
    for j in range(deep):
        got = v[pl.ds(j, 2 * rows, stride=deep), :].T
        values = dot3(halves(got), weights, NN) * (1.0 / (rows * cols))
        for g in range(groups):
            out[g * deep + j] = values[g * qlocal:(g + 1) * qlocal, :]


def solution(mesh):
    nz, ns = mesh.shape["blk"], mesh.shape["sub"]
    devices = nz * ns

    def local(dense, sparse, pattern):
        blocks, qlocal, rows = dense.shape
        cols = qlocal * ns
        per = rows // devices
        chunk = min(per, 2)
        chunks = per // chunk
        entries = sparse.shape[0]
        row_table, sparse_table, twist, dft = tables(rows, cols, devices, chunk)
        depth = 2 * rows * blocks * qlocal // cols
        f32 = jnp.float32
        vmem = pl.BlockSpec(memory_space=pltpu.VMEM)
        sparse_shape = (entries, sparse_table.shape[0], cols)

        def body(*refs):
            kernel(nz, ns, chunk, *refs)

        return pl.pallas_call(
            body,
            out_shape=jax.ShapeDtypeStruct(dense.shape, f32),
            in_specs=[
                vmem, vmem, pl.BlockSpec(memory_space=pltpu.SMEM),
                vmem, vmem, pl.BlockSpec(memory_space=pl.ANY), vmem,
            ],
            out_specs=vmem,
            scratch_shapes=[
                pltpu.VMEM((depth, cols), f32),
                pltpu.VMEM((depth, cols), f32),
                pltpu.VMEM((depth, cols), f32),
                pltpu.VMEM((depth, cols), f32),
                pltpu.VMEM(sparse_shape, f32),
                pltpu.VMEM(sparse_shape, f32),
                pltpu.VMEM((blocks * nz, 2 * cols), f32),
                pltpu.VMEM(twist.shape[1:], f32),
                pltpu.SemaphoreType.DMA((chunks, devices)),
                pltpu.SemaphoreType.DMA((chunks, devices)),
                pltpu.SemaphoreType.DMA((chunks, devices)),
                pltpu.SemaphoreType.DMA((chunks, devices)),
                pltpu.SemaphoreType.DMA((entries, devices)),
                pltpu.SemaphoreType.DMA((entries, devices)),
                pltpu.SemaphoreType.DMA,
            ],
            compiler_params=pltpu.CompilerParams(
                collective_id=0, has_side_effects=True, vmem_limit_bytes=48 * 1024 * 1024
            ),
            cost_estimate=pl.CostEstimate(
                flops=1500000000, bytes_accessed=4000000, transcendentals=0
            ),
            name="series",
        )(dense, sparse, pattern, row_table, sparse_table, twist, dft)

    return jax.shard_map(
        local,
        mesh=mesh,
        in_specs=(
            P(("groups", "blk"), "sub", None),
            P(("groups", "blk"), "sub", None),
            P("groups"),
        ),
        out_specs=P(("groups", "blk"), "sub", None),
        check_vma=False,
    )
```

```python
import numpy as np

import jax
import jax.numpy as jnp
from jax import lax
from jax.experimental import pallas as pl
from jax.experimental.pallas import tpu as pltpu
from jax.sharding import PartitionSpec as P

NN = (((1,), (0,)), ((), ()))
NT = (((1,), (1,)), ((), ()))


def halves(x):
    hi = x.astype(jnp.bfloat16)
    return hi, (x - hi.astype(jnp.float32)).astype(jnp.bfloat16)


def dot3(a, b, dims):
    def one(x, y):
        return lax.dot_general(x, y, dims, preferred_element_type=jnp.float32)

    return one(a[0], b[0]) + (one(a[0], b[1]) + one(a[1], b[0]))


def tables(rows, cols, devices, chunk):
    per = rows // devices
    e = np.arange(rows)
    phase = (np.outer(2 * e + 1, np.arange(rows)) % (4 * rows)) * (2 * np.pi / (4 * rows))
    both = np.stack([np.cos(phase), -np.sin(phase)], axis=1)
    by_device = both.reshape(devices, per // chunk, chunk, 2, rows)
    row_table = by_device.transpose(1, 0, 2, 3, 4).reshape(2 * rows, rows)
    sparse_rows = max(8, 2 * per)
    sparse_table = np.zeros((devices, sparse_rows, rows))
    sparse_table[:, : 2 * per] = both.reshape(devices, 2 * per, rows)
    twist_phase = np.outer(np.arange(cols), 2 * e + 1) * (2 * np.pi / (4 * rows * cols))
    twist = np.stack([np.cos(twist_phase), -np.sin(twist_phase)], axis=2)
    twist = twist.reshape(cols, devices, 2 * per).transpose(1, 0, 2)
    dft_phase = (np.outer(np.arange(cols), np.arange(cols)) % cols) * (2 * np.pi / cols)
    dft = np.concatenate([np.cos(dft_phase), -np.sin(dft_phase)], axis=1)
    out = (row_table, sparse_table.reshape(devices * sparse_rows, rows), twist, dft)
    return [np.asarray(t, np.float32) for t in out]


def kernel(
    nz, ns, chunk,
    dense_far, sparse_far, pattern, row_far, sparse_table_far, twist_far, dft_far,
    out,
    y, r, u, v, ysp, rsp, xs, twist,
    send1, recv1, send2, recv2, send3, recv3,
    dense, sparse, row_table, sparse_table, dft, load_sem,
):
    devices = nz * ns
    blocks, qlocal, rows = dense.shape
    cols = qlocal * ns
    groups = cols // qlocal
    deep = blocks // groups
    per = rows // devices
    chunks = per // chunk
    total = blocks * nz
    span = chunk * 2 * deep
    sparse_rows = rsp.shape[1] // devices
    entries = sparse.shape[0]
    iz, js = lax.axis_index("blk"), lax.axis_index("sub")
    me = iz * ns + js

    loads = [
        pltpu.make_async_copy(far, near, load_sem.at[n])
        for n, (far, near) in enumerate(
            [
                (sparse_table_far, sparse_table), (sparse_far, sparse), (row_far, row_table),
                (dense_far, dense), (twist_far.at[me], twist), (dft_far, dft),
            ]
        )
    ]
    for load in loads:
        load.start()

    def where(i):
        peer = lax.rem(me + i, devices)
        return peer, {"blk": peer // ns, "sub": lax.rem(peer, ns)}

    barrier = pltpu.get_barrier_semaphore()

    @pl.loop(1, devices)
    def _(i):
        pl.semaphore_signal(
            barrier, inc=1, device_id=where(i)[1], device_id_type=pl.DeviceIdType.MESH
        )

    loads[0].wait()
    loads[1].wait()
    for i in range(entries):
        wide = jnp.concatenate([sparse[i]] * groups, axis=0)
        ysp[i] = dot3(halves(sparse_table[...]), halves(wide), NT)

    pl.semaphore_wait(barrier, devices - 1)

    def at(ref, ch, dev):
        return ref.at[pl.ds(pl.multiple_of((ch * devices + dev) * span, span), span), :]

    def move(src, dst, sends, recvs, ch, i):
        peer, ident = where(i)
        return pltpu.make_async_remote_copy(
            src_ref=at(src, ch, peer), dst_ref=at(dst, ch, me),
            send_sem=sends.at[ch, i], recv_sem=recvs.at[ch, i],
            device_id=ident, device_id_type=pl.DeviceIdType.MESH,
        )

    def move_sparse(n, i):
        peer, ident = where(i)

        def part(ref, dev):
            start = pl.multiple_of(dev * sparse_rows, sparse_rows)
            return ref.at[n, pl.ds(start, sparse_rows), :]

        return pltpu.make_async_remote_copy(
            src_ref=part(ysp, peer), dst_ref=part(rsp, me),
            send_sem=send3.at[n, i], recv_sem=recv3.at[n, i],
            device_id=ident, device_id_type=pl.DeviceIdType.MESH,
        )

    for n in range(entries):
        @pl.loop(1, devices)
        def _(i):
            move_sparse(n, i).start()
        own = pl.ds(pl.multiple_of(me * sparse_rows, sparse_rows), sparse_rows)
        rsp[n, own, :] = ysp[n, own, :]

    loads[2].wait()
    loads[3].wait()
    inputs = []
    for j in range(deep):
        inputs.append(halves(jnp.concatenate([dense[g * deep + j] for g in range(groups)], axis=0)))
    slab = devices * chunk * 2
    for ch in range(chunks):
        weights = halves(row_table[ch * slab:(ch + 1) * slab, :])
        for j in range(deep):
            y[pl.ds(ch * slab * deep + j, slab, stride=deep), :] = dot3(weights, inputs[j], NT)

        @pl.loop(1, devices)
        def _(i):
            move(y, r, send1, recv1, ch, i).start()
        own = pl.ds(pl.multiple_of((ch * devices + me) * span, span), span)
        r[own, :] = y[own, :]

    loads[4].wait()
    loads[5].wait()
    for n in range(entries):
        @pl.loop(1, devices)
        def _(i):
            move_sparse(n, i).wait()

    group_of = lax.broadcasted_iota(jnp.int32, (deep, cols), 1) // qlocal
    sub_group = lax.broadcasted_iota(jnp.int32, (ns, cols), 1) // qlocal
    sub_row = lax.broadcasted_iota(jnp.int32, (ns, cols), 0)
    own_lane = sub_group == sub_row

    def regroup(tiles):
        result = []
        for b in range(groups):
            got = None
            for a in range(groups):
                shift = ((a - b) * qlocal) % cols
                piece = pltpu.roll(tiles[a], shift, 1) if shift else tiles[a]
                got = piece if got is None else jnp.where(group_of == a, piece, got)
            result.append(got)
        return result

    for ch in range(chunks):
        @pl.loop(1, devices)
        def _(i):
            move(y, r, send1, recv1, ch, i).wait()

        for e in range(chunk):
            k = ch * chunk + e
            base = (e * 2) * deep
            for c in range(2):
                for z in range(nz):
                    tiles = []
                    for s in range(ns):
                        start = (ch * devices + z * ns + s) * span + base + c * deep
                        tiles.append(r[start:start + deep, :])
                    for g, tile in enumerate(regroup(tiles)):
                        start = z * blocks + g * deep
                        xs[start:start + deep, c * cols:(c + 1) * cols] = tile
            spectra = []
            for z in range(nz):
                for n in range(entries):
                    pair = []
                    for c in range(2):
                        start = z * ns * sparse_rows + 2 * k + c
                        got = rsp[n, pl.ds(start, ns, stride=sparse_rows), :]
                        pair.append(jnp.sum(jnp.where(own_lane, got, 0.0), axis=0, keepdims=True))
                    spectra.append(jnp.concatenate(pair, axis=1))
            count = len(spectra)
            fill = -count % 8
            if fill:
                spectra.append(jnp.zeros((fill, 2 * cols), jnp.float32))
            spectra = jnp.concatenate(spectra, axis=0)

            cos_q = twist[:, 2 * k:2 * k + 1]
            sin_q = twist[:, 2 * k + 1:2 * k + 2]
            base_re, base_im = dft[:, :cols], dft[:, cols:]
            t_re = cos_q * base_re - sin_q * base_im
            t_im = cos_q * base_im + sin_q * base_re
            matrix = halves(
                jnp.concatenate(
                    [
                        jnp.concatenate([t_re, t_im], axis=1),
                        jnp.concatenate([-t_im, t_re], axis=1),
                    ],
                    axis=0,
                )
            )

            x = xs[...]
            before = pltpu.roll(x, 1, 0)
            parity = lax.rem(me * per + k, 2)
            sign = (1 - 2 * parity).astype(jnp.float32)
            turned = jnp.concatenate([-before[:, cols:], before[:, :cols]], axis=1)
            spectrum = dot3(halves(x + sign * turned), matrix, NN)
            sparse_spectrum = dot3(halves(spectra), matrix, NN)
            sum_re = jnp.zeros((total, cols), jnp.float32)
            sum_im = jnp.zeros((total, cols), jnp.float32)
            for n in range(count):
                shift = lax.rem(pattern[n], total)
                a = pltpu.roll(spectrum, shift, 0)
                s_re = sparse_spectrum[n:n + 1, :cols]
                s_im = sparse_spectrum[n:n + 1, cols:]
                sum_re += a[:, :cols] * s_re - a[:, cols:] * s_im
                sum_im += a[:, :cols] * s_im + a[:, cols:] * s_re
            back = dot3(halves(jnp.concatenate([sum_re, sum_im], axis=1)), matrix, NT)
            for c in range(2):
                for z in range(nz):
                    tiles = []
                    for g in range(groups):
                        start = z * blocks + g * deep
                        tiles.append(back[start:start + deep, c * cols:(c + 1) * cols])
                    for s, tile in enumerate(regroup(tiles)):
                        start = (ch * devices + z * ns + s) * span + base + c * deep
                        u[start:start + deep, :] = tile

        @pl.loop(1, devices)
        def _(i):
            move(u, v, send2, recv2, ch, i).start()
        own = pl.ds(pl.multiple_of((ch * devices + me) * span, span), span)
        v[own, :] = u[own, :]

    for ch in range(chunks):
        @pl.loop(1, devices)
        def _(i):
            move(u, v, send2, recv2, ch, i).wait()

    weights = halves(row_table[...])
    for j in range(deep):
        got = v[pl.ds(j, 2 * rows, stride=deep), :].T
        values = dot3(halves(got), weights, NN) * (1.0 / (rows * cols))
        for g in range(groups):
            out[g * deep + j] = values[g * qlocal:(g + 1) * qlocal, :]


def solution(mesh):
    nz, ns = mesh.shape["blk"], mesh.shape["sub"]
    devices = nz * ns

    def local(dense, sparse, pattern):
        blocks, qlocal, rows = dense.shape
        cols = qlocal * ns
        per = rows // devices
        chunk = min(per, 2)
        chunks = per // chunk
        entries = sparse.shape[0]
        row_table, sparse_table, twist, dft = tables(rows, cols, devices, chunk)
        depth = 2 * rows * blocks * qlocal // cols
        f32 = jnp.float32
        vmem = pl.BlockSpec(memory_space=pltpu.VMEM)
        far = pl.BlockSpec(memory_space=pltpu.HBM)
        sparse_shape = (entries, sparse_table.shape[0], cols)

        def body(*refs):
            kernel(nz, ns, chunk, *refs)

        return pl.pallas_call(
            body,
            out_shape=jax.ShapeDtypeStruct(dense.shape, f32),
            in_specs=[
                far, far, pl.BlockSpec(memory_space=pltpu.SMEM),
                far, far, far, far,
            ],
            out_specs=vmem,
            scratch_shapes=[
                pltpu.VMEM((depth, cols), f32),
                pltpu.VMEM((depth, cols), f32),
                pltpu.VMEM((depth, cols), f32),
                pltpu.VMEM((depth, cols), f32),
                pltpu.VMEM(sparse_shape, f32),
                pltpu.VMEM(sparse_shape, f32),
                pltpu.VMEM((blocks * nz, 2 * cols), f32),
                pltpu.VMEM(twist.shape[1:], f32),
                pltpu.SemaphoreType.DMA((chunks, devices)),
                pltpu.SemaphoreType.DMA((chunks, devices)),
                pltpu.SemaphoreType.DMA((chunks, devices)),
                pltpu.SemaphoreType.DMA((chunks, devices)),
                pltpu.SemaphoreType.DMA((entries, devices)),
                pltpu.SemaphoreType.DMA((entries, devices)),
                pltpu.VMEM(dense.shape, f32),
                pltpu.VMEM(sparse.shape, f32),
                pltpu.VMEM(row_table.shape, f32),
                pltpu.VMEM(sparse_table.shape, f32),
                pltpu.VMEM(dft.shape, f32),
                pltpu.SemaphoreType.DMA((6,)),
            ],
            compiler_params=pltpu.CompilerParams(
                collective_id=0, has_side_effects=True, vmem_limit_bytes=64 * 1024 * 1024
            ),
            cost_estimate=pl.CostEstimate(
                flops=1500000000, bytes_accessed=4000000, transcendentals=0
            ),
            name="series",
        )(dense, sparse, pattern, row_table, sparse_table, twist, dft)

    return jax.shard_map(
        local,
        mesh=mesh,
        in_specs=(
            P(("groups", "blk"), "sub", None),
            P(("groups", "blk"), "sub", None),
            P("groups"),
        ),
        out_specs=P(("groups", "blk"), "sub", None),
        check_vma=False,
    )
```
